32 devices in a mesh: parts: 2 (over y), grid: 16 (over z, x, core).
Axes of the slice: x: 2, y: 2, z: 4, core: 2. Of those that a mesh axis runs over, the one named last changes fastest.
Arguments:
- observations: float32 [2048, 40, 1024], P(('parts', 'grid')), parts along dimension 0, may hold values from -16 to 16
- observation_mask: int32 [2048, 40, 1024], P(('parts', 'grid')), parts along dimension 0, may hold values 0 or 1
- noise_class: int32 [2048], P(('parts', 'grid')), parts along dimension 0, may hold values from 0 to 3
- station_kernel: bfloat16 [1024, 1024], replicated, may hold values from -1 to 2, as said below
- time_kernel: bfloat16 [1024, 1024], replicated, may hold values from -1 to 2, as said below
- variable_cov: bfloat16 [40, 40], replicated, may hold values from -1 to 2, as said below
Outputs:
- solution: float32 [2048, 40, 1024], P(('parts', 'grid')), parts along dimension 0
- residual: float32 [2048, 40, 1024], P(('parts', 'grid')), parts along dimension 0
The draws below stay inside these ranges and needn't reach their ends.
There are 2 independent parts, one for each index of `parts`. The reference program is written for one: setup_inputs(seed, part) draws one part's arguments, and reference() takes and returns one part's arrays. A program takes and returns all parts, laid end to end along the dimension named above; an argument that names none is the same for every part. Nothing has to cross between parts.
Inputs may be any that keep to these rules, and one draw needn't show every extreme that they name: `station_kernel`: symmetric. `time_kernel`: symmetric. `variable_cov`: symmetric.
All inputs are finite; a program needn't handle non-finite values. No bound on the sum of `observation_mask` on one device may be relied on, other than what follows from the above.
Results may differ from the reference program's by a relative error of at most 0.0094.
Values may be sent and summed in bfloat16 or wider, within the bound.
A program may use at most 192 MiB of HBM per device.

```python
import jax
import jax.numpy as jnp
from jax import lax

S = 1024
T_SIZE = 1024
V = 40
ITERS = 2


def kernel_draw(key, order):
    raw = jax.random.truncated_normal(key, -4.0, 4.0, (order, order), jnp.float32)
    symmetric = (raw + raw.T) * (0.25 / jnp.sqrt(2.0 * order))
    return (jnp.eye(order, dtype=jnp.float32) + symmetric).astype(jnp.bfloat16)


def draw_station_kernel(key, part):
    return kernel_draw(jax.random.fold_in(key, 11), S)


def draw_time_kernel(key, part):
    return kernel_draw(jax.random.fold_in(key, 23), T_SIZE)


def draw_variable_cov(key, part):
    return kernel_draw(jax.random.fold_in(key, 37), V)


def draw_observations(key, part):
    first_key = jax.random.fold_in(key, 51)
    rising = 1.0 + 0.75 * jnp.arange(S, dtype=jnp.float32) / S
    values = jax.random.truncated_normal(first_key, -4.0, 4.0, (S, V, T_SIZE), jnp.float32)
    scales = rising
    return values * scales[:, None, None]


def touch_ends(result, own_key, least, high):
    longest = result.shape.index(max(result.shape))
    spots = []
    for shift in (0, 1):
        where = [jax.random.randint(jax.random.fold_in(own_key, axis), (), 0, length) for axis, length in enumerate(result.shape)]
        where[longest] = (where[longest] + shift) % result.shape[longest]
        spots.append(tuple(where))
    return result.at[spots[0]].set(least).at[spots[1]].set(high)


def setup_inputs(seed: int = 0, part: int = 0) -> dict:
    splits = jax.random.split(jax.random.key(seed), 7)
    part_splits = jax.random.split(jax.random.fold_in(splits[6], part), 7)
    return {
        "observations": draw_observations(jax.random.fold_in(jax.random.fold_in(splits[6], part), 71), part),
        "observation_mask": touch_ends((jax.random.randint(part_splits[1], (S, V, T_SIZE), 0, 4) < 3).astype(jnp.int32), jax.random.fold_in(part_splits[1], 1), 0, 1),
        "noise_class": touch_ends(jax.random.randint(part_splits[2], (S,), 0, 4), jax.random.fold_in(part_splits[2], 1), 0, 3).astype(jnp.int32),
        "station_kernel": draw_station_kernel(jax.random.fold_in(splits[6], 71), part),
        "time_kernel": draw_time_kernel(jax.random.fold_in(splits[6], 71), part),
        "variable_cov": draw_variable_cov(jax.random.fold_in(splits[6], 71), part),
    }


noise_levels = (0.05, 0.2, 0.6, 1.5)


def operator(vector, station_kernel, time_kernel, variable_cov, mask_float, noise_cells):
    highest = lax.Precision.HIGHEST
    rounded = vector.astype(jnp.bfloat16).astype(jnp.float32)
    mixed = jnp.einsum('wv,svt->swt', variable_cov.astype(jnp.float32), rounded, precision=highest)
    mixed = mixed.astype(jnp.bfloat16).astype(jnp.float32)
    timed = jnp.einsum('svt,ut->svu', mixed, time_kernel.astype(jnp.float32), precision=highest)
    timed = timed.astype(jnp.bfloat16).astype(jnp.float32)
    spaced = jnp.einsum('rs,svt->rvt', station_kernel.astype(jnp.float32), timed, precision=highest)
    spaced = spaced.astype(jnp.bfloat16).astype(jnp.float32)
    return mask_float * spaced + noise_cells * vector


def reference(observations, observation_mask, noise_class, station_kernel, time_kernel, variable_cov):
    table = jnp.array(noise_levels, dtype=jnp.float32)
    noise_cells = table[noise_class][:, None, None]
    mask_float = observation_mask.astype(jnp.float32)
    target = mask_float * observations
    solution = jnp.zeros_like(target)
    residual = target
    for inner_index in range(ITERS):
        image = operator(residual, station_kernel, time_kernel, variable_cov, mask_float, noise_cells)
        norm_sq = jnp.sum(residual * residual)
        curvature = jnp.sum(residual * image)
        step_size = norm_sq / curvature
        solution = solution + step_size * residual
        residual = residual - step_size * image
    return solution, residual
```

```python
import math

import jax
import jax.numpy as jnp
from jax import lax
from jax.sharding import PartitionSpec as P

ITERS = 2


noise_levels = (0.05, 0.2, 0.6, 1.5)


def body(observations, observation_mask, noise_class, station_kernel, time_kernel, variable_cov):
    devices = lax.axis_size("grid")
    stations, variables, length = observations.shape
    all_stations = station_kernel.shape[0]
    columns = variables * length // devices
    lane = math.gcd(math.gcd(128, columns), length)
    tiles = length // lane
    chunk = columns // lane
    levels = jnp.zeros((stations,), jnp.float32)
    for level_index, level_value in enumerate(noise_levels):
        levels = levels + jnp.where(noise_class == level_index, level_value, 0.0)
    noise_cells = levels[:, None, None]
    mask_float = observation_mask.astype(jnp.float32)
    target = mask_float * observations
    solution = jnp.zeros_like(target)
    residual = target
    for inner_index in range(ITERS):
        rounded = residual.astype(jnp.bfloat16)
        mixed = jnp.einsum(
            "wv,svt->swt", variable_cov, rounded, preferred_element_type=jnp.float32
        ).astype(jnp.bfloat16)
        timed = jnp.einsum(
            "wst,ut->wsu", jnp.transpose(mixed, (1, 0, 2)), time_kernel, preferred_element_type=jnp.float32
        ).astype(jnp.bfloat16)
        pieces = timed.reshape(variables, stations, tiles, lane)
        pieces = jnp.transpose(pieces, (0, 2, 1, 3)).reshape(devices, chunk, stations, lane)
        gathered = lax.all_to_all(pieces, "grid", split_axis=0, concat_axis=0, tiled=True)
        gathered = jnp.transpose(gathered, (0, 2, 1, 3)).reshape(all_stations, chunk * lane)
        spaced = jnp.einsum(
            "rs,sk->rk", station_kernel, gathered, preferred_element_type=jnp.float32
        ).astype(jnp.bfloat16)
        spaced = jnp.transpose(spaced.reshape(devices, stations, chunk, lane), (0, 2, 1, 3))
        spaced = lax.all_to_all(spaced, "grid", split_axis=0, concat_axis=0, tiled=True)
        spaced = jnp.transpose(spaced.reshape(variables, tiles, stations, lane), (2, 0, 1, 3))
        spaced = spaced.reshape(stations, variables, length).astype(jnp.float32)
        image = mask_float * spaced + noise_cells * residual
        norm_sq, curvature = lax.psum((jnp.sum(residual * residual), jnp.sum(residual * image)), "grid")
        step_size = norm_sq / curvature
        solution, residual = (solution + step_size * residual, residual - step_size * image)
    return (solution, residual)


def solution(mesh):
    return jax.shard_map(
        body,
        mesh=mesh,
        in_specs=(
            P(("parts", "grid"), None, None),
            P(("parts", "grid"), None, None),
            P(("parts", "grid")),
            P(),
            P(),
            P(),
        ),
        out_specs=(P(("parts", "grid"), None, None), P(("parts", "grid"), None, None)),
        check_vma=False,
    )
```

```python
import functools
import math

import jax
import jax.numpy as jnp
from jax import lax
from jax.experimental import pallas as pl
from jax.experimental.pallas import tpu as pltpu
from jax.sharding import PartitionSpec as P

ITERS = 2


noise_levels = (0.05, 0.2, 0.6, 1.5)


MESH = pl.DeviceIdType.MESH


def greet(devices, me):
    barrier = pltpu.get_barrier_semaphore()

    def signal(k, carry):
        pl.semaphore_signal(barrier, inc=1, device_id={"grid": lax.rem(me + k, devices)}, device_id_type=MESH)
        return carry

    lax.fori_loop(1, devices, signal, 0)
    pl.semaphore_wait(barrier, devices - 1)


def operator_kernel(
    mixed_ref, time_ref, station_ref, out_ref, pieces, held, result, out_send, out_recv, back_send, back_recv, own_out, own_back
):
    groups, devices, per, stations, lane = held.shape
    tiles = time_ref.shape[1] // lane
    group_variables = mixed_ref.shape[0] // groups
    me = lax.axis_index("grid")

    def outward(g, k, owner):
        peer = lax.rem(me + k, devices)
        return pltpu.make_async_remote_copy(
            src_ref=pieces.at[g, peer],
            dst_ref=held.at[g, owner],
            send_sem=out_send.at[g, k - 1],
            recv_sem=out_recv.at[g, k - 1],
            device_id={"grid": peer},
            device_id_type=MESH,
        )

    def homeward(g, k, owner):
        peer = lax.rem(me + k, devices)
        return pltpu.make_async_remote_copy(
            src_ref=result.at[g, peer],
            dst_ref=out_ref.at[g, owner],
            send_sem=back_send.at[g, k - 1],
            recv_sem=back_recv.at[g, k - 1],
            device_id={"grid": peer},
            device_id_type=MESH,
        )

    def stay_out(g):
        return pltpu.make_async_copy(pieces.at[g, me], held.at[g, me], own_out.at[g])

    def stay_back(g):
        return pltpu.make_async_copy(result.at[g, me], out_ref.at[g, me], own_back.at[g])

    def over(body):
        def step(k, carry):
            body(k, lax.rem(me + devices - k, devices))
            return carry

        lax.fori_loop(1, devices, step, 0)

    greet(devices, me)

    def send_group(g, carry):
        rows = mixed_ref[pl.ds(g * group_variables, group_variables)]
        rows = rows.reshape(group_variables * stations, tiles * lane)
        timed = jnp.dot(rows, time_ref[...], preferred_element_type=jnp.float32).astype(jnp.bfloat16)
        for v in range(group_variables):
            for tile in range(tiles):
                block = v * tiles + tile
                pieces[g, block // per, block % per] = timed[
                    v * stations : (v + 1) * stations, tile * lane : (tile + 1) * lane
                ]
        stay_out(g).start()
        over(lambda k, source: outward(g, k, me).start())
        return carry

    lax.fori_loop(0, groups, send_group, 0)

    def contract_group(g, carry):
        stay_out(g).wait()
        over(lambda k, source: outward(g, k, source).wait_recv())
        values = jnp.concatenate(
            [held[g, :, index].reshape(devices * stations, lane) for index in range(per)], axis=1
        )
        product = jnp.dot(station_ref[...], values, preferred_element_type=jnp.float32).astype(jnp.bfloat16)
        for index in range(per):
            result[g, :, index] = product[:, index * lane : (index + 1) * lane].reshape(devices, stations, lane)
        stay_back(g).start()
        over(lambda k, source: homeward(g, k, me).start())
        return carry

    lax.fori_loop(0, groups, contract_group, 0)

    def finish_group(g, carry):
        stay_back(g).wait()
        over(lambda k, source: homeward(g, k, source).wait_recv())
        over(lambda k, source: outward(g, k, source).wait_send())
        over(lambda k, source: homeward(g, k, source).wait_send())
        return carry

    lax.fori_loop(0, groups, finish_group, 0)


def apply_operator(mixed, time_kernel, station_kernel, devices, groups, per, lane):
    variables, stations, length = mixed.shape
    blocks = (groups, devices, per, stations, lane)
    remote = pltpu.SemaphoreType.DMA((groups, devices - 1))
    own = pltpu.SemaphoreType.DMA((groups,))
    return pl.pallas_call(
        operator_kernel,
        out_shape=jax.ShapeDtypeStruct(blocks, jnp.bfloat16),
        in_specs=[pl.BlockSpec(memory_space=pltpu.VMEM)] * 3,
        out_specs=pl.BlockSpec(memory_space=pl.ANY),
        scratch_shapes=[pltpu.VMEM(blocks, jnp.bfloat16)] * 3 + [remote] * 4 + [own] * 2,
        compiler_params=pltpu.CompilerParams(
            collective_id=0, has_side_effects=True, vmem_limit_bytes=48 * 2**20
        ),
        cost_estimate=pl.CostEstimate(
            flops=2 * variables * stations * length * (length + devices * stations),
            bytes_accessed=4 * variables * stations * length,
            transcendentals=0,
        ),
    )(mixed, time_kernel, station_kernel)


def total_kernel(devices, mine_ref, out_ref, held, send, recv):
    me = lax.axis_index("grid")

    def copy(k, owner):
        peer = lax.rem(me + k, devices)
        return pltpu.make_async_remote_copy(
            src_ref=mine_ref,
            dst_ref=held.at[owner],
            send_sem=send.at[k - 1],
            recv_sem=recv.at[k - 1],
            device_id={"grid": peer},
            device_id_type=MESH,
        )

    greet(devices, me)

    def start(k, carry):
        copy(k, me).start()
        return carry

    def end(k, carry):
        copy(k, lax.rem(me + devices - k, devices)).wait()
        return carry

    lax.fori_loop(1, devices, start, 0)
    held[me] = mine_ref[...]
    lax.fori_loop(1, devices, end, 0)
    out_ref[...] = jnp.sum(held[...], axis=0)


def grid_totals(first, second, devices):
    mine = jnp.where(lax.broadcasted_iota(jnp.int32, (8, 128), 0) == 0, first, second)
    sums = pl.pallas_call(
        functools.partial(total_kernel, devices),
        out_shape=jax.ShapeDtypeStruct((8, 128), jnp.float32),
        in_specs=[pl.BlockSpec(memory_space=pltpu.VMEM)],
        out_specs=pl.BlockSpec(memory_space=pltpu.VMEM),
        scratch_shapes=[
            pltpu.VMEM((devices, 8, 128), jnp.float32),
            pltpu.SemaphoreType.DMA((devices - 1,)),
            pltpu.SemaphoreType.DMA((devices - 1,)),
        ],
        compiler_params=pltpu.CompilerParams(collective_id=1, has_side_effects=True),
    )(mine)
    return sums[0, 0], sums[1, 0]


def body(observations, observation_mask, noise_class, station_kernel, time_kernel, variable_cov):
    devices = lax.axis_size("grid")
    stations, variables, length = observations.shape
    all_stations = station_kernel.shape[0]
    columns = variables * length // devices
    lane = math.gcd(math.gcd(128, columns), length)
    tiles = length // lane
    chunk = columns // lane
    groups = 5
    per = chunk // groups
    plain = lane < 128 or stations % 16 != 0 or chunk % groups != 0 or variables % groups != 0
    levels = jnp.zeros((stations,), jnp.float32)
    for level_index, level_value in enumerate(noise_levels):
        levels = levels + jnp.where(noise_class == level_index, level_value, 0.0)
    noise_cells = levels[:, None, None]
    mask_float = observation_mask.astype(jnp.float32)
    target = mask_float * observations
    solution = jnp.zeros_like(target)
    residual = target
    for inner_index in range(ITERS):
        rounded = residual.astype(jnp.bfloat16)
        mixed = jnp.einsum(
            "wv,svt->swt", variable_cov, rounded, preferred_element_type=jnp.float32
        ).astype(jnp.bfloat16)
        mixed = jnp.transpose(mixed, (1, 0, 2))
        if plain:
            timed = jnp.einsum(
                "wst,ut->wsu", mixed, time_kernel, preferred_element_type=jnp.float32
            ).astype(jnp.bfloat16)
            pieces = timed.reshape(variables, stations, tiles, lane)
            pieces = jnp.transpose(pieces, (0, 2, 1, 3)).reshape(devices, chunk, stations, lane)
            gathered = lax.all_to_all(pieces, "grid", split_axis=0, concat_axis=0, tiled=True)
            spaced = jnp.einsum(
                "arbs,bcsl->acrl",
                station_kernel.reshape(devices, stations, devices, stations),
                gathered,
                preferred_element_type=jnp.float32,
            ).astype(jnp.bfloat16)
            spaced = lax.all_to_all(spaced, "grid", split_axis=0, concat_axis=0, tiled=True)
        else:
            spaced = apply_operator(mixed, time_kernel, station_kernel, devices, groups, per, lane)
        spaced = jnp.transpose(spaced.reshape(variables, tiles, stations, lane), (0, 2, 1, 3))
        spaced = lax.optimization_barrier(spaced.reshape(variables, stations, length))
        spaced = lax.optimization_barrier(jnp.transpose(spaced, (1, 0, 2)))
        spaced = spaced.astype(jnp.float32)
        image = mask_float * spaced + noise_cells * residual
        norm_sq, curvature = jnp.sum(residual * residual), jnp.sum(residual * image)
        if plain:
            norm_sq, curvature = lax.psum((norm_sq, curvature), "grid")
        else:
            norm_sq, curvature = grid_totals(norm_sq, curvature, devices)
        step_size = norm_sq / curvature
        solution, residual = (solution + step_size * residual, residual - step_size * image)
    return (solution, residual)


def solution(mesh):
    return jax.shard_map(
        body,
        mesh=mesh,
        in_specs=(
            P(("parts", "grid"), None, None),
            P(("parts", "grid"), None, None),
            P(("parts", "grid")),
            P(),
            P(),
            P(),
        ),
        out_specs=(P(("parts", "grid"), None, None), P(("parts", "grid"), None, None)),
        check_vma=False,
    )
```

```python
import functools
import math

import jax
import jax.numpy as jnp
from jax import lax
from jax.experimental import pallas as pl
from jax.experimental.layout import Layout, with_layout_constraint
from jax.experimental.pallas import tpu as pltpu
from jax.sharding import PartitionSpec as P

ITERS = 2


noise_levels = (0.05, 0.2, 0.6, 1.5)


MESH = pl.DeviceIdType.MESH


def greet(devices, me):
    barrier = pltpu.get_barrier_semaphore()

    def signal(k, carry):
        pl.semaphore_signal(barrier, inc=1, device_id={"grid": lax.rem(me + k, devices)}, device_id_type=MESH)
        return carry

    lax.fori_loop(1, devices, signal, 0)
    pl.semaphore_wait(barrier, devices - 1)


def operator_kernel(
    mixed_ref, time_ref, station_ref, out_ref, pieces, held, result, out_send, out_recv, back_send, back_recv, own_out, own_back
):
    groups, devices, stations, width = held.shape
    spans = time_ref.shape[1] // width
    group_variables = mixed_ref.shape[0] // groups
    me = lax.axis_index("grid")

    def outward(g, k, owner):
        peer = lax.rem(me + k, devices)
        return pltpu.make_async_remote_copy(
            src_ref=pieces.at[g, peer],
            dst_ref=held.at[g, owner],
            send_sem=out_send.at[g, k - 1],
            recv_sem=out_recv.at[g, k - 1],
            device_id={"grid": peer},
            device_id_type=MESH,
        )

    def place(g, owner):
        variable = g * group_variables + owner // spans
        start = pl.multiple_of(lax.rem(owner, spans) * width, width)
        return out_ref.at[variable, :, pl.ds(start, width)]

    def homeward(g, k, owner):
        peer = lax.rem(me + k, devices)
        return pltpu.make_async_remote_copy(
            src_ref=result.at[g, peer],
            dst_ref=place(g, owner),
            send_sem=back_send.at[g, k - 1],
            recv_sem=back_recv.at[g, k - 1],
            device_id={"grid": peer},
            device_id_type=MESH,
        )

    def stay_out(g):
        return pltpu.make_async_copy(pieces.at[g, me], held.at[g, me], own_out.at[g])

    def stay_back(g):
        return pltpu.make_async_copy(result.at[g, me], place(g, me), own_back.at[g])

    def over(body):
        def step(k, carry):
            body(k, lax.rem(me + devices - k, devices))
            return carry

        lax.fori_loop(1, devices, step, 0)

    greet(devices, me)

    def send_group(g, carry):
        rows = mixed_ref[pl.ds(g * group_variables, group_variables)]
        rows = rows.reshape(group_variables * stations, spans * width)
        timed = jnp.dot(rows, time_ref[...], preferred_element_type=jnp.float32).astype(jnp.bfloat16)
        for v in range(group_variables):
            for span in range(spans):
                pieces[g, v * spans + span] = timed[
                    v * stations : (v + 1) * stations, span * width : (span + 1) * width
                ]
        stay_out(g).start()
        over(lambda k, source: outward(g, k, me).start())
        return carry

    lax.fori_loop(0, groups, send_group, 0)

    def contract_group(g, carry):
        stay_out(g).wait()
        over(lambda k, source: outward(g, k, source).wait_recv())
        values = held[g].reshape(devices * stations, width)
        product = jnp.dot(station_ref[...], values, preferred_element_type=jnp.float32).astype(jnp.bfloat16)
        result[g] = product.reshape(devices, stations, width)
        stay_back(g).start()
        over(lambda k, source: homeward(g, k, me).start())
        return carry

    lax.fori_loop(0, groups, contract_group, 0)

    def finish_group(g, carry):
        stay_back(g).wait()
        over(lambda k, source: homeward(g, k, source).wait_recv())
        over(lambda k, source: outward(g, k, source).wait_send())
        over(lambda k, source: homeward(g, k, source).wait_send())
        return carry

    lax.fori_loop(0, groups, finish_group, 0)


def apply_operator(mixed, time_kernel, station_kernel, devices, groups, width):
    variables, stations, length = mixed.shape
    blocks = (groups, devices, stations, width)
    remote = pltpu.SemaphoreType.DMA((groups, devices - 1))
    own = pltpu.SemaphoreType.DMA((groups,))
    return pl.pallas_call(
        operator_kernel,
        out_shape=jax.ShapeDtypeStruct(mixed.shape, jnp.bfloat16),
        in_specs=[pl.BlockSpec(memory_space=pltpu.VMEM)] * 3,
        out_specs=pl.BlockSpec(memory_space=pl.ANY),
        scratch_shapes=[pltpu.VMEM(blocks, jnp.bfloat16)] * 3 + [remote] * 4 + [own] * 2,
        compiler_params=pltpu.CompilerParams(
            collective_id=0, has_side_effects=True, vmem_limit_bytes=40 * 2**20
        ),
        cost_estimate=pl.CostEstimate(
            flops=2 * variables * stations * length * (length + devices * stations),
            bytes_accessed=4 * variables * stations * length,
            transcendentals=0,
        ),
    )(mixed, time_kernel, station_kernel)


def total_kernel(devices, mine_ref, out_ref, held, send, recv):
    me = lax.axis_index("grid")

    def copy(k, owner):
        peer = lax.rem(me + k, devices)
        return pltpu.make_async_remote_copy(
            src_ref=mine_ref,
            dst_ref=held.at[owner],
            send_sem=send.at[k - 1],
            recv_sem=recv.at[k - 1],
            device_id={"grid": peer},
            device_id_type=MESH,
        )

    greet(devices, me)

    def start(k, carry):
        copy(k, me).start()
        return carry

    def end(k, carry):
        copy(k, lax.rem(me + devices - k, devices)).wait()
        return carry

    lax.fori_loop(1, devices, start, 0)
    held[me] = mine_ref[...]
    lax.fori_loop(1, devices, end, 0)
    out_ref[...] = jnp.sum(held[...], axis=0)


def grid_totals(first, second, devices):
    mine = jnp.where(lax.broadcasted_iota(jnp.int32, (8, 128), 0) == 0, first, second)
    sums = pl.pallas_call(
        functools.partial(total_kernel, devices),
        out_shape=jax.ShapeDtypeStruct((8, 128), jnp.float32),
        in_specs=[pl.BlockSpec(memory_space=pltpu.VMEM)],
        out_specs=pl.BlockSpec(memory_space=pltpu.VMEM),
        scratch_shapes=[
            pltpu.VMEM((devices, 8, 128), jnp.float32),
            pltpu.SemaphoreType.DMA((devices - 1,)),
            pltpu.SemaphoreType.DMA((devices - 1,)),
        ],
        compiler_params=pltpu.CompilerParams(collective_id=1, has_side_effects=True),
    )(mine)
    return sums[0, 0], sums[1, 0]


def body(observations, observation_mask, noise_class, station_kernel, time_kernel, variable_cov):
    devices = lax.axis_size("grid")
    stations, variables, length = observations.shape
    all_stations = station_kernel.shape[0]
    columns = variables * length // devices
    lane = math.gcd(math.gcd(128, columns), length)
    tiles = length // lane
    chunk = columns // lane
    groups = 5
    per = max(chunk // groups, 1)
    plain = lane < 128 or stations % 16 != 0 or variables % groups != 0 or chunk % groups != 0 or tiles % per != 0
    levels = jnp.zeros((stations,), jnp.float32)
    for level_index, level_value in enumerate(noise_levels):
        levels = levels + jnp.where(noise_class == level_index, level_value, 0.0)
    noise_cells = levels[:, None, None]
    mask_float = observation_mask.astype(jnp.float32)
    target = mask_float * observations
    solution = jnp.zeros_like(target)
    residual = target
    for inner_index in range(ITERS):
        rounded = residual.astype(jnp.bfloat16)
        mixed = jnp.einsum(
            "wv,svt->swt", variable_cov, rounded, preferred_element_type=jnp.float32
        ).astype(jnp.bfloat16)
        mixed = jnp.transpose(mixed, (1, 0, 2))
        if plain:
            timed = jnp.einsum(
                "wst,ut->wsu", mixed, time_kernel, preferred_element_type=jnp.float32
            ).astype(jnp.bfloat16)
            pieces = timed.reshape(variables, stations, tiles, lane)
            pieces = jnp.transpose(pieces, (0, 2, 1, 3)).reshape(devices, chunk, stations, lane)
            gathered = lax.all_to_all(pieces, "grid", split_axis=0, concat_axis=0, tiled=True)
            spaced = jnp.einsum(
                "arbs,bcsl->acrl",
                station_kernel.reshape(devices, stations, devices, stations),
                gathered,
                preferred_element_type=jnp.float32,
            ).astype(jnp.bfloat16)
            spaced = lax.all_to_all(spaced, "grid", split_axis=0, concat_axis=0, tiled=True)
            spaced = jnp.transpose(spaced.reshape(variables, tiles, stations, lane), (0, 2, 1, 3))
            spaced = spaced.reshape(variables, stations, length)
        else:
            spaced = apply_operator(mixed, time_kernel, station_kernel, devices, groups, per * lane)
        spaced = with_layout_constraint(jnp.transpose(spaced, (1, 0, 2)), Layout((0, 1, 2)))
        spaced = spaced.astype(jnp.float32)
        image = mask_float * spaced + noise_cells * residual
        norm_sq = jnp.sum(residual * residual)
        curvature = jnp.sum(residual * (spaced + noise_cells * residual))
        if plain:
            norm_sq, curvature = lax.psum((norm_sq, curvature), "grid")
        else:
            norm_sq, curvature = grid_totals(norm_sq, curvature, devices)
        step_size = norm_sq / curvature
        solution, residual = (solution + step_size * residual, residual - step_size * image)
    return (solution, residual)


def solution(mesh):
    return jax.shard_map(
        body,
        mesh=mesh,
        in_specs=(
            P(("parts", "grid"), None, None),
            P(("parts", "grid"), None, None),
            P(("parts", "grid")),
            P(),
            P(),
            P(),
        ),
        out_specs=(P(("parts", "grid"), None, None), P(("parts", "grid"), None, None)),
        check_vma=False,
    )
```

```python
import functools
import math

import jax
import jax.numpy as jnp
from jax import lax
from jax.experimental import pallas as pl
from jax.experimental.layout import Layout, with_layout_constraint
from jax.experimental.pallas import tpu as pltpu
from jax.sharding import PartitionSpec as P

ITERS = 2


noise_levels = (0.05, 0.2, 0.6, 1.5)


MESH = pl.DeviceIdType.MESH


def greet(devices, me):
    barrier = pltpu.get_barrier_semaphore()

    def signal(k, carry):
        pl.semaphore_signal(barrier, inc=1, device_id={"grid": lax.rem(me + k, devices)}, device_id_type=MESH)
        return carry

    lax.fori_loop(1, devices, signal, 0)
    pl.semaphore_wait(barrier, devices - 1)


def operator_kernel(
    mixed_ref, time_ref, station_ref, out_ref, pieces, held, result, out_send, out_recv, back_send, back_recv, own_out, own_back
):
    groups, devices, stations, width = held.shape
    spans = time_ref.shape[1] // width
    group_variables = mixed_ref.shape[0] // groups
    me = lax.axis_index("grid")

    def outward(g, k, owner):
        peer = lax.rem(me + k, devices)
        return pltpu.make_async_remote_copy(
            src_ref=pieces.at[g, peer],
            dst_ref=held.at[g, owner],
            send_sem=out_send.at[g, k - 1],
            recv_sem=out_recv.at[g, k - 1],
            device_id={"grid": peer},
            device_id_type=MESH,
        )

    def place(g, owner):
        variable = g * group_variables + owner // spans
        start = pl.multiple_of(lax.rem(owner, spans) * width, width)
        return out_ref.at[variable, :, pl.ds(start, width)]

    def homeward(g, k, owner):
        peer = lax.rem(me + k, devices)
        return pltpu.make_async_remote_copy(
            src_ref=result.at[g, peer],
            dst_ref=place(g, owner),
            send_sem=back_send.at[g, k - 1],
            recv_sem=back_recv.at[g, k - 1],
            device_id={"grid": peer},
            device_id_type=MESH,
        )

    def stay_out(g):
        return pltpu.make_async_copy(pieces.at[g, me], held.at[g, me], own_out.at[g])

    def stay_back(g):
        return pltpu.make_async_copy(result.at[g, me], place(g, me), own_back.at[g])

    def over(body):
        def step(k, carry):
            body(k, lax.rem(me + devices - k, devices))
            return carry

        lax.fori_loop(1, devices, step, 0)

    greet(devices, me)

    def send_group(g, carry):
        rows = mixed_ref[pl.ds(g * group_variables, group_variables)]
        rows = rows.reshape(group_variables * stations, spans * width)
        timed = jnp.dot(rows, time_ref[...], preferred_element_type=jnp.float32).astype(jnp.bfloat16)
        for v in range(group_variables):
            for span in range(spans):
                pieces[g, v * spans + span] = timed[
                    v * stations : (v + 1) * stations, span * width : (span + 1) * width
                ]
        stay_out(g).start()
        over(lambda k, source: outward(g, k, me).start())
        return carry

    lax.fori_loop(0, groups, send_group, 0)

    def contract_group(g, carry):
        stay_out(g).wait()
        over(lambda k, source: outward(g, k, source).wait_recv())
        values = held[g].reshape(devices * stations, width)
        product = jnp.dot(station_ref[...], values, preferred_element_type=jnp.float32).astype(jnp.bfloat16)
        result[g] = product.reshape(devices, stations, width)
        stay_back(g).start()
        over(lambda k, source: homeward(g, k, me).start())
        return carry

    lax.fori_loop(0, groups, contract_group, 0)

    def finish_group(g, carry):
        stay_back(g).wait()
        over(lambda k, source: homeward(g, k, source).wait_recv())
        over(lambda k, source: outward(g, k, source).wait_send())
        over(lambda k, source: homeward(g, k, source).wait_send())
        return carry

    lax.fori_loop(0, groups, finish_group, 0)


def apply_operator(mixed, time_kernel, station_kernel, devices, groups, width):
    variables, stations, length = mixed.shape
    blocks = (groups, devices, stations, width)
    remote = pltpu.SemaphoreType.DMA((groups, devices - 1))
    own = pltpu.SemaphoreType.DMA((groups,))
    return pl.pallas_call(
        operator_kernel,
        out_shape=jax.ShapeDtypeStruct(mixed.shape, jnp.bfloat16),
        in_specs=[pl.BlockSpec(memory_space=pltpu.VMEM)] * 3,
        out_specs=pl.BlockSpec(memory_space=pl.ANY),
        scratch_shapes=[pltpu.VMEM(blocks, jnp.bfloat16)] * 3 + [remote] * 4 + [own] * 2,
        compiler_params=pltpu.CompilerParams(
            collective_id=0, has_side_effects=True, vmem_limit_bytes=40 * 2**20
        ),
        cost_estimate=pl.CostEstimate(
            flops=2 * variables * stations * length * (length + devices * stations),
            bytes_accessed=4 * variables * stations * length,
            transcendentals=0,
        ),
    )(mixed, time_kernel, station_kernel)


def total_kernel(devices, mine_ref, out_ref, held, send, recv):
    me = lax.axis_index("grid")

    def copy(k, owner):
        peer = lax.rem(me + k, devices)
        return pltpu.make_async_remote_copy(
            src_ref=mine_ref,
            dst_ref=held.at[owner],
            send_sem=send.at[k - 1],
            recv_sem=recv.at[k - 1],
            device_id={"grid": peer},
            device_id_type=MESH,
        )

    greet(devices, me)

    def start(k, carry):
        copy(k, me).start()
        return carry

    def end(k, carry):
        copy(k, lax.rem(me + devices - k, devices)).wait()
        return carry

    lax.fori_loop(1, devices, start, 0)
    held[me] = mine_ref[...]
    lax.fori_loop(1, devices, end, 0)
    out_ref[...] = jnp.sum(held[...], axis=0)


def grid_totals(first, second, devices):
    mine = jnp.where(lax.broadcasted_iota(jnp.int32, (8, 128), 0) == 0, first, second)
    sums = pl.pallas_call(
        functools.partial(total_kernel, devices),
        out_shape=jax.ShapeDtypeStruct((8, 128), jnp.float32),
        in_specs=[pl.BlockSpec(memory_space=pltpu.VMEM)],
        out_specs=pl.BlockSpec(memory_space=pltpu.VMEM),
        scratch_shapes=[
            pltpu.VMEM((devices, 8, 128), jnp.float32),
            pltpu.SemaphoreType.DMA((devices - 1,)),
            pltpu.SemaphoreType.DMA((devices - 1,)),
        ],
        compiler_params=pltpu.CompilerParams(collective_id=1, has_side_effects=True),
    )(mine)
    return sums[0, 0], sums[1, 0]


def body(observations, observation_mask, noise_class, station_kernel, time_kernel, variable_cov):
    devices = lax.axis_size("grid")
    stations, variables, length = observations.shape
    all_stations = station_kernel.shape[0]
    columns = variables * length // devices
    lane = math.gcd(math.gcd(128, columns), length)
    tiles = length // lane
    chunk = columns // lane
    groups = 10
    per = max(chunk // groups, 1)
    plain = lane < 128 or stations % 16 != 0 or variables % groups != 0 or chunk % groups != 0 or tiles % per != 0
    levels = jnp.zeros((stations,), jnp.float32)
    for level_index, level_value in enumerate(noise_levels):
        levels = levels + jnp.where(noise_class == level_index, level_value, 0.0)
    noise_cells = levels[:, None, None]
    mask_float = observation_mask.astype(jnp.float32)
    target = mask_float * observations
    solution = jnp.zeros_like(target)
    residual = target
    for inner_index in range(ITERS):
        rounded = residual.astype(jnp.bfloat16)
        mixed = jnp.einsum(
            "wv,svt->swt", variable_cov, rounded, preferred_element_type=jnp.float32
        ).astype(jnp.bfloat16)
        mixed = jnp.transpose(mixed, (1, 0, 2))
        if plain:
            timed = jnp.einsum(
                "wst,ut->wsu", mixed, time_kernel, preferred_element_type=jnp.float32
            ).astype(jnp.bfloat16)
            pieces = timed.reshape(variables, stations, tiles, lane)
            pieces = jnp.transpose(pieces, (0, 2, 1, 3)).reshape(devices, chunk, stations, lane)
            gathered = lax.all_to_all(pieces, "grid", split_axis=0, concat_axis=0, tiled=True)
            spaced = jnp.einsum(
                "arbs,bcsl->acrl",
                station_kernel.reshape(devices, stations, devices, stations),
                gathered,
                preferred_element_type=jnp.float32,
            ).astype(jnp.bfloat16)
            spaced = lax.all_to_all(spaced, "grid", split_axis=0, concat_axis=0, tiled=True)
            spaced = jnp.transpose(spaced.reshape(variables, tiles, stations, lane), (0, 2, 1, 3))
            spaced = spaced.reshape(variables, stations, length)
        else:
            spaced = apply_operator(mixed, time_kernel, station_kernel, devices, groups, per * lane)
        spaced = with_layout_constraint(jnp.transpose(spaced, (1, 0, 2)), Layout((0, 1, 2)))
        spaced = spaced.astype(jnp.float32)
        image = mask_float * spaced + noise_cells * residual
        norm_sq = jnp.sum(residual * residual)
        curvature = jnp.sum(residual * (spaced + noise_cells * residual))
        if plain:
            norm_sq, curvature = lax.psum((norm_sq, curvature), "grid")
        else:
            norm_sq, curvature = grid_totals(norm_sq, curvature, devices)
        step_size = norm_sq / curvature
        solution, residual = (solution + step_size * residual, residual - step_size * image)
    return (solution, residual)


def solution(mesh):
    return jax.shard_map(
        body,
        mesh=mesh,
        in_specs=(
            P(("parts", "grid"), None, None),
            P(("parts", "grid"), None, None),
            P(("parts", "grid")),
            P(),
            P(),
            P(),
        ),
        out_specs=(P(("parts", "grid"), None, None), P(("parts", "grid"), None, None)),
        check_vma=False,
    )
```
